256 devices in a mesh: island: 8 (over y, core), shard: 32 (over x, z).
Axes of the slice: x: 4, y: 4, z: 8, core: 2. Of those that a mesh axis runs over, the one named last changes fastest.
Arguments:
- pseudo_grad: float32 [8, 8192, 4096], P('island', 'shard'), may hold values from -6 to 6
- error_buffer: float32 [8, 8192, 4096], P('island', 'shard'), may hold values from -6 to 6
- momentum: float32 [8192, 4096], P('shard'), may hold values from -4 to 4
- weights: bfloat16 [8192, 4096], P('shard'), may hold values from -6 to 6
- warm_basis: float32 [8192, 64], P('shard'), may hold values from -6 to 6
Outputs:
- new_error: float32 [8, 8192, 4096], P('island', 'shard')
- new_momentum: float32 [8192, 4096], P('shard')
- new_weights: bfloat16 [8192, 4096], P('shard')
- new_basis: float32 [8192, 64], P('shard')
The draws below stay inside these ranges and needn't reach their ends.
All inputs are finite; a program needn't handle non-finite values.
Results may differ from the reference program's by a relative error of at most 0.001.
Values sent between devices are 32-bit elements; how exact they have to be, the bound alone decides.
No kernel may reach another device: no remote copies, remote signals or barrier semaphores. Data moves between devices by JAX's collectives and lax.ppermute only.
A program may use at most 128 MiB of HBM per device.

```python
import jax
import jax.numpy as jnp
from jax import lax

D = 4096
RANK = 64
ITERS = 2
FF = 8192
N_ISLAND = 8


def level_of(key, dims, pieces, least, largest):
    factor_of = 1.0
    for position, shards_of in pieces:
        draws = jax.random.uniform(jax.random.fold_in(jax.random.fold_in(key, 6), position), (shards_of,), jnp.float32, least / len(pieces), largest / len(pieces))
        factor_of = factor_of * jnp.repeat(jnp.exp(draws), dims[position] // shards_of).reshape((-1,) + (1,) * (len(dims) - 1 - position))
    return factor_of


def bell_draw(rng, dims, deviation, limit, split=(), kind=jnp.bfloat16):
    level = level_of(rng, dims, split, -0.22, 0.18) if split else 1.0
    array = jax.random.normal(rng, dims, jnp.float32) * deviation * level
    return jnp.minimum(jnp.maximum(array, -limit), limit).astype(kind)


def setup_inputs(seed: int = 0) -> dict:
    arg_keys = jax.random.split(jax.random.key(seed), 6)
    return {
        "pseudo_grad": bell_draw(arg_keys[0], (N_ISLAND, FF, D), 1.0, 6.0, ((0, 8), (1, 32)), jnp.float32),
        "error_buffer": bell_draw(arg_keys[1], (N_ISLAND, FF, D), 0.5, 6.0, ((0, 8), (1, 32)), jnp.float32),
        "momentum": bell_draw(arg_keys[2], (FF, D), 0.3, 4.0, ((0, 32),), jnp.float32),
        "weights": bell_draw(arg_keys[3], (FF, D), 1.0, 6.0, ((0, 32),)),
        "warm_basis": bell_draw(arg_keys[4], (FF, RANK), 1.0, 6.0, ((0, 32),), jnp.float32),
    }


HIGH = lax.Precision.HIGHEST
outer_beta = 0.9
outer_rate = 0.7

def orthonormal(factor_rows):
    gram_matrix = jnp.dot(factor_rows, factor_rows.T, precision=HIGH)
    lower_factor = jnp.linalg.cholesky(gram_matrix)
    return lax.linalg.triangular_solve(lower_factor, factor_rows, left_side=True, lower=True)

def reference(pseudo_grad, error_buffer, momentum, weights, warm_basis):
    merged = pseudo_grad + error_buffer
    summed = jnp.sum(merged, axis=0)
    basis_now = warm_basis
    for iteration in range(ITERS):
        factor_rows = orthonormal(jnp.dot(basis_now.T, summed, precision=HIGH))
        local_proj = jnp.einsum('ifd,rd->ifr', merged, factor_rows, precision=HIGH)
        basis_now = jnp.sum(local_proj, axis=0)
    new_error = merged - jnp.einsum('ifr,rd->ifd', local_proj, factor_rows, precision=HIGH)
    update = jnp.dot(basis_now / N_ISLAND, factor_rows, precision=HIGH)
    new_momentum = outer_beta * momentum + update
    stepped = weights.astype(jnp.float32) - outer_rate * (update + outer_beta * new_momentum)
    return (new_error, new_momentum, stepped.astype(jnp.bfloat16), basis_now)
```

```python
import jax
import jax.numpy as jnp
from jax import lax
from jax.sharding import Mesh, PartitionSpec as P

ITERS = 2

HIGHEST = lax.Precision.HIGHEST
HIGH = lax.Precision.HIGH
outer_beta = 0.9
outer_rate = 0.7
SIBLING = [(0, 1), (1, 0)]


def at(pieces, index):
    return lax.dynamic_index_in_dim(pieces, index, 0, keepdims=False)


def around(axis, distance):
    size = lax.axis_size(axis)
    return [(i, (i + distance) % size) for i in range(size)]


def scattered_sum(pieces, axis):
    size = lax.axis_size(axis)
    me = lax.axis_index(axis)
    arrived = [
        lax.ppermute(at(pieces, (me + d) % size), axis, around(axis, d)) for d in range(1, size)
    ]
    total = at(pieces, me)
    for piece in arrived:
        total = total + piece
    return total


def gathered(piece, axis):
    size = lax.axis_size(axis)
    me = lax.axis_index(axis)
    arrived = [lax.ppermute(piece, axis, around(axis, d)) for d in range(1, size)]
    out = jnp.zeros((size, *piece.shape), piece.dtype)
    out = lax.dynamic_update_index_in_dim(out, piece, me, 0)
    for d, other in zip(range(1, size), arrived):
        out = lax.dynamic_update_index_in_dim(out, other, (me - d) % size, 0)
    return out


def summed_directly(value, axis):
    size = lax.axis_size(axis)
    arrived = [lax.ppermute(value, axis, around(axis, d)) for d in range(1, size)]
    total = value
    for other in arrived:
        total = total + other
    return total


def summed_everywhere(blocks):
    ranks, width = blocks.shape[1:]
    pieces = blocks.reshape(2, 16, ranks, width)
    pieces = scattered_sum(pieces, "core").reshape(4, 4, ranks, width)
    pieces = scattered_sum(pieces, "y")
    piece = scattered_sum(pieces, "x")
    size = lax.axis_size("z")
    copies = jnp.broadcast_to(piece[None], (size, *piece.shape))
    piece = lax.all_to_all(copies, "z", 0, 0, tiled=True).sum(axis=0)
    pieces = gathered(piece, "x")
    pieces = gathered(pieces, "y")
    pieces = gathered(pieces, "core")
    return pieces.reshape(blocks.shape)


def over_island(value):
    return summed_directly(summed_directly(value, "core"), "y")


def inverse_factor(factor_rows):
    gram = lax.dot_general(factor_rows, factor_rows, (((0, 2), (0, 2)), ((), ())), precision=HIGHEST)
    lower = jnp.linalg.cholesky(gram)
    eye = jnp.eye(gram.shape[0], dtype=gram.dtype)
    return lax.linalg.triangular_solve(lower, eye, left_side=True, lower=True)


def on_device(pseudo_grad, error_buffer, momentum, weights, warm_basis):
    merged = (pseudo_grad + error_buffer)[0]
    rows, columns = merged.shape
    basis_t = warm_basis.T
    blocked = merged.reshape(rows, 32, columns // 32)
    for iteration in range(ITERS):
        partial_blocks = lax.dot_general(blocked, basis_t, (((0,), (1,)), ((), ())), precision=HIGH)
        factor = summed_everywhere(partial_blocks.transpose(0, 2, 1))
        proj_t = lax.dot_general(factor, blocked, (((0, 2), (1, 2)), ((), ())), precision=HIGH)
        summed_t = over_island(proj_t)
        inverse = inverse_factor(factor)
        basis_t = jnp.dot(inverse, summed_t, precision=HIGHEST)
    local_t = jnp.dot(inverse, proj_t, precision=HIGHEST)
    flat = factor.transpose(1, 0, 2).reshape(-1, columns)
    factor_rows = jnp.dot(inverse, flat, precision=HIGHEST)
    new_error = merged - lax.dot_general(local_t, factor_rows, (((0,), (0,)), ((), ())), precision=HIGH)
    update = lax.dot_general(basis_t / 8, factor_rows, (((0,), (0,)), ((), ())), precision=HIGH)
    new_momentum = outer_beta * momentum + update
    stepped = weights.astype(jnp.float32) - outer_rate * (update + outer_beta * new_momentum)
    return (new_error[None], new_momentum, stepped.astype(jnp.bfloat16), basis_t.T)


def solution(mesh):
    grid = Mesh(mesh.devices.reshape(4, 2, 4, 8), ("y", "core", "x", "z"))
    island, shard = ("y", "core"), ("x", "z")
    in_specs = (
        P(island, shard, None),
        P(island, shard, None),
        P(shard, None),
        P(shard, None),
        P(shard, None),
    )
    out_specs = (P(island, shard, None), P(shard, None), P(shard, None), P(shard, None))
    return jax.shard_map(
        on_device, mesh=grid, in_specs=in_specs, out_specs=out_specs, check_vma=False
    )
```

```python
import jax
import jax.numpy as jnp
from jax import lax
from jax.experimental import pallas as pl
from jax.experimental.pallas import tpu as pltpu
from jax.sharding import Mesh, PartitionSpec as P

HIGHEST = lax.Precision.HIGHEST
F32, BF16 = jnp.float32, jnp.bfloat16
outer_beta = 0.9
outer_rate = 0.7
SIBLING = [(0, 1), (1, 0)]
LANES = 128
WIDE = 1024
PER = WIDE // LANES


def halves(value):
    high = value.astype(BF16)
    return high, (value - high.astype(F32)).astype(BF16)


def dot(a, b, dims=((1,), (0,)), precision=None):
    return lax.dot_general(a, b, (dims, ((), ())), precision=precision, preferred_element_type=F32)


def joined(blocks_ref):
    return jnp.concatenate([blocks_ref[j] for j in range(PER)], axis=1)


def put_blocks(out_ref, value):
    for j in range(PER):
        out_ref[j] = value[:, j * LANES : (j + 1) * LANES]


def rank_product(basis_t, high, low):
    basis_high, basis_low = halves(basis_t)
    ranks = basis_t.shape[0]
    both = dot(jnp.concatenate([basis_high, basis_low], axis=0), high)
    return both[:ranks] + both[ranks:] + dot(basis_high, low)


def stacked_columns(factor_t):
    high, low = halves(factor_t.T)
    return jnp.concatenate([high, low, high], axis=1)


def first_kernel(grad_ref, error_ref, basis_ref, high_ref, low_ref, partial_ref):
    high, low = halves(grad_ref[0] + error_ref[0])
    high_ref[...] = high
    low_ref[...] = low
    put_blocks(partial_ref, rank_product(basis_ref[...], high, low))


def partial_kernel(high_ref, low_ref, summed_ref, inverse_ref, partial_ref, basis_ref):
    @pl.when(pl.program_id(0) == 0)
    def _():
        basis_ref[...] = dot(inverse_ref[...], summed_ref[...], precision=HIGHEST)

    put_blocks(partial_ref, rank_product(basis_ref[...], high_ref[...], low_ref[...]))


def proj_kernel(factor_ref, high_ref, low_ref, out_ref):
    @pl.when(pl.program_id(0) == 0)
    def _():
        out_ref[...] = jnp.zeros_like(out_ref)

    high, low = halves(joined(factor_ref))
    ranks = high.shape[0]
    across = ((1,), (1,))
    both = dot(jnp.concatenate([high, low], axis=0), high_ref[...], across)
    out_ref[...] += both[:ranks] + both[ranks:] + dot(high, low_ref[...], across)


def error_kernel(high_ref, low_ref, factor_ref, proj_ref, inverse_ref, error_ref, rows_ref, left_ref):
    @pl.when(pl.program_id(0) == 0)
    def _():
        left_ref[...] = stacked_columns(dot(inverse_ref[...], proj_ref[...], precision=HIGHEST))

    high, low = halves(dot(inverse_ref[...], joined(factor_ref), precision=HIGHEST))
    rows = jnp.concatenate([high, high, low], axis=0)
    rows_ref[...] = rows
    merged = high_ref[...].astype(F32) + low_ref[...].astype(F32)
    error_ref[0] = merged - dot(left_ref[...], rows)


def step_kernel(rows_ref, momentum_ref, weights_ref, summed_ref, inverse_ref, new_momentum_ref, new_weights_ref, basis_ref, left_ref):
    @pl.when(pl.program_id(0) == 0)
    def _():
        basis = dot(inverse_ref[...], summed_ref[...], precision=HIGHEST)
        basis_ref[...] = basis
        left_ref[...] = stacked_columns(basis * 0.125)

    update = dot(left_ref[...], rows_ref[...])
    new_momentum = outer_beta * momentum_ref[...] + update
    new_momentum_ref[...] = new_momentum
    stepped = weights_ref[...].astype(F32) - outer_rate * (update + outer_beta * new_momentum)
    new_weights_ref[...] = stepped.astype(BF16)


def wide(rows):
    return pl.BlockSpec((rows, WIDE), lambda i: (0, i))


def whole(*shape):
    return pl.BlockSpec(shape, lambda i: (0,) * len(shape))


def replica(rows):
    return pl.BlockSpec((1, rows, WIDE), lambda i: (0, 0, i))


def blocks(ranks):
    return pl.BlockSpec((PER, ranks, LANES), lambda i: (i, 0, 0))


def call(kernel, columns, in_specs, outs, scratch=(), flops=0, traffic=0, limit=24):
    shapes = [jax.ShapeDtypeStruct(shape, kind) for shape, kind, _ in outs]
    specs = [spec for _, _, spec in outs]
    return pl.pallas_call(
        kernel,
        grid=(columns // WIDE,),
        in_specs=in_specs,
        out_shape=shapes,
        out_specs=specs,
        scratch_shapes=list(scratch),
        compiler_params=pltpu.CompilerParams(vmem_limit_bytes=limit * 2**20),
        cost_estimate=pl.CostEstimate(flops=flops, bytes_accessed=traffic, transcendentals=0),
    )


def at(pieces, index):
    return lax.dynamic_index_in_dim(pieces, index, 0, keepdims=False)


def around(axis, distance):
    size = lax.axis_size(axis)
    return [(i, (i + distance) % size) for i in range(size)]


def summed_directly(value, axis):
    size = lax.axis_size(axis)
    arrived = [lax.ppermute(value, axis, around(axis, d)) for d in range(1, size)]
    total = value
    for other in arrived:
        total = total + other
    return total


def to_everyone(piece, axes):
    size = lax.axis_size(axes)
    copies = jnp.broadcast_to(piece[None], (size, *piece.shape))
    return lax.all_to_all(copies, axes, 0, 0, tiled=True)


def summed_everywhere(pieces):
    count, ranks, width = pieces.shape
    core = lax.axis_index("core")
    pieces = pieces.reshape(2, count // 2, ranks, width)
    pieces = at(pieces, core) + lax.ppermute(at(pieces, 1 - core), "core", SIBLING)
    piece = lax.all_to_all(pieces, ("y", "x"), 0, 0, tiled=True).sum(axis=0)
    piece = to_everyone(piece, "z").sum(axis=0)
    pieces = to_everyone(piece, ("y", "x"))
    other = lax.ppermute(pieces, "core", SIBLING)
    out = jnp.zeros((2, *pieces.shape), pieces.dtype)
    out = lax.dynamic_update_index_in_dim(out, pieces, core, 0)
    out = lax.dynamic_update_index_in_dim(out, other, 1 - core, 0)
    return out.reshape(count, ranks, width)


def over_island(value):
    paired = summed_directly(value, "core")
    return paired, summed_directly(paired, "y")


def spread(tile, column):
    return jnp.broadcast_to(tile[:, column : column + 1], tile.shape)


def inverse_kernel(factor_ref, anchor_ref, out_ref):
    ranks = factor_ref.shape[1]
    gram = jnp.zeros((ranks, ranks), F32)
    for q in range(0, factor_ref.shape[0], 4):
        part = jnp.concatenate([factor_ref[q + j] for j in range(4)], axis=1)
        gram += dot(part, part, ((1,), (1,)), HIGHEST)
    row = lax.broadcasted_iota(jnp.int32, (ranks, ranks), 0)
    diagonal = row == lax.broadcasted_iota(jnp.int32, (ranks, ranks), 1)
    kept = jnp.where(diagonal, gram, 0.0)
    across = lax.rsqrt(jnp.sum(kept, axis=0, keepdims=True))
    down = lax.rsqrt(jnp.sum(kept, axis=1, keepdims=True))
    work = jnp.concatenate([gram * down * across, jnp.where(diagonal, across, 0.0)], axis=1)
    tiles = [work[8 * t : 8 * t + 8] for t in range(ranks // 8)]
    row = lax.broadcasted_iota(jnp.int32, (8, 2 * ranks), 0)
    out = []
    for j in range(0, ranks, 2):
        t, s = divmod(j, 8)
        left, right = spread(tiles[t], j), spread(tiles[t], j + 1)
        top, low = tiles[t][s : s + 1], tiles[t][s + 1 : s + 2]
        a, b, d = left[s : s + 1], left[s + 1 : s + 2], right[s + 1 : s + 2]
        det = a * d - b * b
        over = 1.0 / det
        rest = a * low - b * top
        first = (d * top - b * low) * over
        second = rest * over
        out.append(top * lax.rsqrt(a))
        out.append(rest * lax.rsqrt(a * det))
        for k in range(t, ranks // 8):
            if k > t:
                left, right = spread(tiles[k], j), spread(tiles[k], j + 1)
            elif s < 6:
                left = jnp.where(row > s + 1, left, 0.0)
                right = jnp.where(row > s + 1, right, 0.0)
            else:
                continue
            tiles[k] = tiles[k] - left * first - right * second
    out_ref[...] = jnp.concatenate(out, axis=0)[:, ranks:]


def inverse_factor(factor, anchor):
    ranks = factor.shape[1]
    return pl.pallas_call(
        inverse_kernel,
        in_specs=[pl.BlockSpec(memory_space=pltpu.VMEM), pl.BlockSpec(memory_space=pl.ANY)],
        out_shape=jax.ShapeDtypeStruct((ranks, ranks), F32),
        compiler_params=pltpu.CompilerParams(vmem_limit_bytes=8 * 2**20),
        cost_estimate=pl.CostEstimate(flops=2 * 10**9, bytes_accessed=2**21, transcendentals=0),
    )(factor, anchor)


def on_device(pseudo_grad, error_buffer, momentum, weights, warm_basis):
    _, rows, columns = pseudo_grad.shape
    ranks = warm_basis.shape[1]
    count = columns // LANES
    flops = 6 * rows * columns * ranks
    size = 4 * rows * columns
    half = ((rows, columns), BF16, wide(rows))
    partial_out = ((count, ranks, LANES), F32, blocks(ranks))
    short = whole(ranks, rows)
    square = whole(ranks, ranks)

    high, low, partial_blocks = call(
        first_kernel,
        columns,
        [replica(rows), replica(rows), short],
        [half, half, partial_out],
        flops=flops,
        traffic=3 * size,
        limit=56,
    )(pseudo_grad, error_buffer, warm_basis.T)
    project = call(
        proj_kernel,
        columns,
        [blocks(ranks), wide(rows), wide(rows)],
        [((ranks, rows), F32, short)],
        flops=flops,
        traffic=size,
    )
    factor = summed_everywhere(partial_blocks)
    (proj_t,) = project(factor, high, low)
    paired, summed_t = over_island(proj_t)
    inverse = inverse_factor(factor, paired)
    (partial_blocks,) = call(
        partial_kernel,
        columns,
        [wide(rows), wide(rows), short, square],
        [partial_out],
        [pltpu.VMEM((ranks, rows), F32)],
        flops=flops,
        traffic=size,
    )(high, low, summed_t, inverse)
    factor = summed_everywhere(partial_blocks)
    (proj_t,) = project(factor, high, low)
    paired, summed_t = over_island(proj_t)
    inverse = inverse_factor(factor, paired)
    new_error, factor_rows = call(
        error_kernel,
        columns,
        [wide(rows), wide(rows), blocks(ranks), short, square],
        [
            ((1, rows, columns), F32, replica(rows)),
            ((3 * ranks, columns), BF16, wide(3 * ranks)),
        ],
        [pltpu.VMEM((rows, 3 * ranks), BF16)],
        flops=flops,
        traffic=2 * size,
    )(high, low, factor, proj_t, inverse)
    new_momentum, new_weights, basis_t = call(
        step_kernel,
        columns,
        [wide(3 * ranks), wide(rows), wide(rows), short, square],
        [
            ((rows, columns), F32, wide(rows)),
            ((rows, columns), BF16, wide(rows)),
            ((ranks, rows), F32, short),
        ],
        [pltpu.VMEM((rows, 3 * ranks), BF16)],
        flops=flops,
        traffic=3 * size,
    )(factor_rows, momentum, weights, summed_t, inverse)
    return new_error, new_momentum, new_weights, basis_t.T


def solution(mesh):
    grid = Mesh(mesh.devices.reshape(4, 2, 4, 8), ("y", "core", "x", "z"))
    island, shard = ("y", "core"), ("x", "z")
    in_specs = (
        P(island, shard, None),
        P(island, shard, None),
        P(shard, None),
        P(shard, None),
        P(shard, None),
    )
    out_specs = (P(island, shard, None), P(shard, None), P(shard, None), P(shard, None))
    return jax.shard_map(
        on_device, mesh=grid, in_specs=in_specs, out_specs=out_specs, check_vma=False
    )
```

```python
import jax
import jax.numpy as jnp
from jax import lax
from jax.experimental import pallas as pl
from jax.experimental.pallas import tpu as pltpu
from jax.sharding import Mesh, PartitionSpec as P

HIGHEST = lax.Precision.HIGHEST
F32, BF16 = jnp.float32, jnp.bfloat16
outer_beta = 0.9
outer_rate = 0.7
SIBLING = [(0, 1), (1, 0)]
LANES = 128
WIDE = 1024
PER = WIDE // LANES
CHUNK = 512


def halves(value):
    high = value.astype(BF16)
    return high, (value - high.astype(F32)).astype(BF16)


def dot(a, b, dims=((1,), (0,)), precision=None):
    return lax.dot_general(a, b, (dims, ((), ())), precision=precision, preferred_element_type=F32)


def joined(blocks_ref):
    return jnp.concatenate([blocks_ref[j] for j in range(PER)], axis=1)


def put_blocks(out_ref, value):
    for j in range(PER):
        out_ref[j] = value[:, j * LANES : (j + 1) * LANES]


def rank_product(basis_t, high, low):
    basis_high, basis_low = halves(basis_t)
    ranks = basis_t.shape[0]
    both = dot(jnp.concatenate([basis_high, basis_low], axis=0), high)
    return both[:ranks] + both[ranks:] + dot(basis_high, low)


def stacked_columns(factor_t):
    high, low = halves(factor_t.T)
    return jnp.concatenate([high, low, high], axis=1)


def first_kernel(grad_ref, error_ref, basis_ref, high_ref, low_ref, away_ref, kept_ref, given_ref, grads, errors, highs, lows, basis, sems):
    columns = grad_ref.shape[2]
    count = columns // CHUNK
    core = lax.axis_index("core")
    start = pltpu.make_async_copy(basis_ref, basis, sems.at[5, 0])
    start.start()
    copies = []
    for c in range(count):
        here = slice(c * CHUNK, (c + 1) * CHUNK)
        pair = [
            pltpu.make_async_copy(source.at[0, :, here], target.at[:, here], sems.at[i, c])
            for i, (source, target) in enumerate(((grad_ref, grads), (error_ref, errors)))
        ]
        for copy in pair:
            copy.start()
        copies.append(pair)
    leaving = []
    start.wait()
    for c, pair in enumerate(copies):
        here = slice(c * CHUNK, (c + 1) * CHUNK)
        for copy in pair:
            copy.wait()
        merged = grads[:, here] + errors[:, here]
        high, low = halves(merged)
        highs[:, here] = high
        lows[:, here] = low
        grads[:, here] = merged
        for i, (source, target) in enumerate(((highs, high_ref), (lows, low_ref))):
            copy = pltpu.make_async_copy(source.at[:, here], target.at[:, here], sems.at[2 + i, c])
            copy.start()
            leaving.append(copy)
        partial = rank_product(basis[...], high, low)
        side, place = divmod(c, count // 2)
        there = slice(place * CHUNK, (place + 1) * CHUNK)
        first = place * (CHUNK // LANES)

        def put(ref):
            for j in range(CHUNK // LANES):
                ref[first + j] = partial[:, j * LANES : (j + 1) * LANES]

        @pl.when(core == side)
        def _():
            put(kept_ref)

        @pl.when(core != side)
        def _():
            put(given_ref)
            pltpu.make_async_copy(grads.at[:, here], away_ref.at[:, there], sems.at[4, place]).start()

    for copy in leaving:
        copy.wait()
    for place in range(count // 2):
        there = slice(place * CHUNK, (place + 1) * CHUNK)
        pltpu.make_async_copy(grads.at[:, there], away_ref.at[:, there], sems.at[4, place]).wait()


def partial_kernel(high_ref, low_ref, summed_ref, inverse_ref, partial_ref, basis_ref):
    @pl.when(pl.program_id(0) == 0)
    def _():
        basis_ref[...] = dot(inverse_ref[...], summed_ref[...], precision=HIGHEST)

    put_blocks(partial_ref, rank_product(basis_ref[...], high_ref[...], low_ref[...]))


def add_projection(factor, high, low, out_ref, gram_ref):
    @pl.when(pl.program_id(0) == 0)
    def _():
        out_ref[...] = jnp.zeros_like(out_ref)
        gram_ref[...] = jnp.zeros_like(gram_ref)

    across = ((1,), (1,))
    factor_high, factor_low = halves(factor)
    ranks = factor.shape[0]
    both = dot(jnp.concatenate([factor_high, factor_low], axis=0), high, across)
    out_ref[...] += both[:ranks] + both[ranks:] + dot(factor_high, low, across)
    gram_ref[...] += dot(factor, factor, across, HIGHEST)


def paired_kernel(core_ref, factor_ref, high_ref, low_ref, arrived_ref, out_ref, high_out, low_out, gram_ref):
    merged = high_ref[...].astype(F32) + low_ref[...].astype(F32)
    high, low = halves(merged + arrived_ref[...])
    high_out[...] = high
    low_out[...] = low
    rows = high.shape[0]
    ranks = factor_ref.shape[1]
    add_projection(joined(factor_ref), high, low, out_ref.at[:, :rows], gram_ref)

    @pl.when(pl.program_id(0) == pl.num_programs(0) - 1)
    def _():
        out_ref[:, rows:] = jnp.concatenate([gram_ref[...], jnp.zeros((ranks, LANES - ranks), F32)], axis=1)


def proj_kernel(factor_ref, high_ref, low_ref, out_ref, gram_ref):
    add_projection(joined(factor_ref), high_ref[...], low_ref[...], out_ref, gram_ref)


def error_kernel(high_ref, low_ref, factor_ref, proj_ref, inverse_ref, error_ref, rows_ref, left_ref):
    @pl.when(pl.program_id(0) == 0)
    def _():
        left_ref[...] = stacked_columns(dot(inverse_ref[...], proj_ref[...], precision=HIGHEST))

    high, low = halves(dot(inverse_ref[...], joined(factor_ref), precision=HIGHEST))
    rows = jnp.concatenate([high, high, low], axis=0)
    rows_ref[...] = rows
    merged = high_ref[...].astype(F32) + low_ref[...].astype(F32)
    error_ref[0] = merged - dot(left_ref[...], rows)


def step_kernel(rows_ref, momentum_ref, weights_ref, summed_ref, inverse_ref, new_momentum_ref, new_weights_ref, basis_ref, left_ref):
    @pl.when(pl.program_id(0) == 0)
    def _():
        basis = dot(inverse_ref[...], summed_ref[...], precision=HIGHEST)
        basis_ref[...] = basis
        left_ref[...] = stacked_columns(basis * 0.125)

    update = dot(left_ref[...], rows_ref[...])
    new_momentum = outer_beta * momentum_ref[...] + update
    new_momentum_ref[...] = new_momentum
    stepped = weights_ref[...].astype(F32) - outer_rate * (update + outer_beta * new_momentum)
    new_weights_ref[...] = stepped.astype(BF16)


def wide(rows):
    return pl.BlockSpec((rows, WIDE), lambda i: (0, i))


def whole(*shape):
    return pl.BlockSpec(shape, lambda i: (0,) * len(shape))


def replica(rows):
    return pl.BlockSpec((1, rows, WIDE), lambda i: (0, 0, i))


def blocks(ranks):
    return pl.BlockSpec((PER, ranks, LANES), lambda i: (i, 0, 0))


def call(kernel, columns, in_specs, outs, scratch=(), flops=0, traffic=0, limit=24):
    shapes = [jax.ShapeDtypeStruct(shape, kind) for shape, kind, _ in outs]
    specs = [spec for _, _, spec in outs]
    return pl.pallas_call(
        kernel,
        grid=(columns // WIDE,),
        in_specs=in_specs,
        out_shape=shapes,
        out_specs=specs,
        scratch_shapes=list(scratch),
        compiler_params=pltpu.CompilerParams(vmem_limit_bytes=limit * 2**20),
        cost_estimate=pl.CostEstimate(flops=flops, bytes_accessed=traffic, transcendentals=0),
    )


def around(axis, distance):
    size = lax.axis_size(axis)
    return [(i, (i + distance) % size) for i in range(size)]


def summed_directly(value, axis):
    size = lax.axis_size(axis)
    arrived = [lax.ppermute(value, axis, around(axis, d)) for d in range(1, size)]
    total = value
    for other in arrived:
        total = total + other
    return total


def to_everyone(piece, axes):
    size = lax.axis_size(axes)
    copies = jnp.broadcast_to(piece[None], (size, *piece.shape))
    return lax.all_to_all(copies, axes, 0, 0, tiled=True)


def over_chips(pieces):
    piece = lax.all_to_all(pieces, ("y", "x"), 0, 0, tiled=True).sum(axis=0)
    piece = to_everyone(piece, "z").sum(axis=0)
    return to_everyone(piece, ("y", "x"))


def both_halves(pieces):
    core = lax.axis_index("core")
    other = lax.ppermute(pieces, "core", SIBLING)
    out = jnp.zeros((2, *pieces.shape), pieces.dtype)
    out = lax.dynamic_update_index_in_dim(out, pieces, core, 0)
    out = lax.dynamic_update_index_in_dim(out, other, 1 - core, 0)
    return out.reshape(-1, *pieces.shape[1:])


def spread(tile, column):
    return jnp.broadcast_to(tile[:, column : column + 1], tile.shape)


def inverse_kernel(gram_ref, anchor_ref, out_ref):
    ranks = out_ref.shape[0]
    gram = gram_ref[:, :ranks]
    row = lax.broadcasted_iota(jnp.int32, (ranks, ranks), 0)
    diagonal = row == lax.broadcasted_iota(jnp.int32, (ranks, ranks), 1)
    kept = jnp.where(diagonal, gram, 0.0)
    across = lax.rsqrt(jnp.sum(kept, axis=0, keepdims=True))
    down = lax.rsqrt(jnp.sum(kept, axis=1, keepdims=True))
    work = jnp.concatenate([gram * down * across, jnp.where(diagonal, across, 0.0)], axis=1)
    tiles = [work[8 * t : 8 * t + 8] for t in range(ranks // 8)]
    row = lax.broadcasted_iota(jnp.int32, (8, 2 * ranks), 0)
    out = []
    for j in range(0, ranks, 2):
        t, s = divmod(j, 8)
        left, right = spread(tiles[t], j), spread(tiles[t], j + 1)
        top, low = tiles[t][s : s + 1], tiles[t][s + 1 : s + 2]
        a, b, d = left[s : s + 1], left[s + 1 : s + 2], right[s + 1 : s + 2]
        det = a * d - b * b
        over = 1.0 / det
        rest = a * low - b * top
        first = (d * top - b * low) * over
        second = rest * over
        out.append(top * lax.rsqrt(a))
        out.append(rest * lax.rsqrt(a * det))
        for k in range(t, ranks // 8):
            if k > t:
                left, right = spread(tiles[k], j), spread(tiles[k], j + 1)
            elif s < 6:
                left = jnp.where(row > s + 1, left, 0.0)
                right = jnp.where(row > s + 1, right, 0.0)
            else:
                continue
            tiles[k] = tiles[k] - left * first - right * second
    out_ref[...] = jnp.concatenate(out, axis=0)[:, ranks:]


def inverse_factor(gram, anchor, block=0):
    ranks, width = gram.shape
    return pl.pallas_call(
        inverse_kernel,
        grid=(1,),
        in_specs=[
            pl.BlockSpec((ranks, min(width, LANES)), lambda i: (0, block)),
            pl.BlockSpec(memory_space=pl.ANY),
        ],
        out_specs=pl.BlockSpec((ranks, ranks), lambda i: (0, 0)),
        out_shape=jax.ShapeDtypeStruct((ranks, ranks), F32),
        compiler_params=pltpu.CompilerParams(vmem_limit_bytes=8 * 2**20),
        cost_estimate=pl.CostEstimate(flops=2 * 10**9, bytes_accessed=2**20, transcendentals=0),
    )(gram, anchor)


def first_product(pseudo_grad, error_buffer, basis_t):
    _, rows, columns = pseudo_grad.shape
    ranks = basis_t.shape[0]
    count = columns // LANES // 2
    in_vmem = pl.BlockSpec(memory_space=pltpu.VMEM)
    in_hbm = pl.BlockSpec(memory_space=pltpu.HBM)
    part = jax.ShapeDtypeStruct((count, ranks, LANES), F32)
    half = pltpu.HBM((rows, columns), BF16)
    return pl.pallas_call(
        first_kernel,
        in_specs=[in_hbm] * 3,
        out_shape=[half, half, pltpu.HBM((rows, columns // 2), F32), part, part],
        out_specs=[in_hbm] * 3 + [in_vmem] * 2,
        scratch_shapes=[
            pltpu.VMEM((rows, columns), F32),
            pltpu.VMEM((rows, columns), F32),
            pltpu.VMEM((rows, columns), BF16),
            pltpu.VMEM((rows, columns), BF16),
            pltpu.VMEM((ranks, rows), F32),
            pltpu.SemaphoreType.DMA((6, columns // CHUNK)),
        ],
        compiler_params=pltpu.CompilerParams(vmem_limit_bytes=24 * 2**20),
        cost_estimate=pl.CostEstimate(
            flops=6 * rows * columns * ranks, bytes_accessed=12 * rows * columns, transcendentals=0
        ),
    )(*(pltpu.with_memory_space_constraint(x, pltpu.HBM) for x in (pseudo_grad, error_buffer, basis_t)))


def paired_product(core, factor, high, low, arrived):
    count, ranks, _ = factor.shape
    rows, half = arrived.shape
    steps = half // WIDE
    mine = pl.BlockSpec((rows, WIDE), lambda i, core: (0, core[0] * steps + i))
    here = pl.BlockSpec((rows, WIDE), lambda i, core: (0, i))
    share = jax.ShapeDtypeStruct((rows, half), BF16)
    return pl.pallas_call(
        paired_kernel,
        grid_spec=pltpu.PrefetchScalarGridSpec(
            num_scalar_prefetch=1,
            grid=(steps,),
            in_specs=[pl.BlockSpec((PER, ranks, LANES), lambda i, core: (i, 0, 0)), mine, mine, here],
            out_specs=[pl.BlockSpec((ranks, rows + LANES), lambda i, core: (0, 0)), here, here],
            scratch_shapes=[pltpu.VMEM((ranks, ranks), F32)],
        ),
        out_shape=[jax.ShapeDtypeStruct((ranks, rows + LANES), F32), share, share],
        compiler_params=pltpu.CompilerParams(vmem_limit_bytes=24 * 2**20),
        cost_estimate=pl.CostEstimate(
            flops=6 * rows * half * ranks, bytes_accessed=12 * rows * half, transcendentals=0
        ),
    )(core, factor, high, pltpu.with_memory_space_constraint(low, pltpu.HBM), arrived)


def on_device(pseudo_grad, error_buffer, momentum, weights, warm_basis):
    _, rows, columns = pseudo_grad.shape
    ranks = warm_basis.shape[1]
    count = columns // LANES
    flops = 6 * rows * columns * ranks
    size = 4 * rows * columns
    short = whole(ranks, rows)
    square = whole(ranks, ranks)
    core = lax.axis_index("core").astype(jnp.int32).reshape(1)

    high, low, away, kept, given = first_product(pseudo_grad, error_buffer, warm_basis.T)
    kept = kept + lax.ppermute(given, "core", SIBLING)
    kept, away = lax.optimization_barrier((kept, away))
    arrived = lax.ppermute(away, "core", SIBLING)
    factor = over_chips(kept)
    proj_t, high_half, low_half = paired_product(core, factor, high, low, arrived)
    paired = summed_directly(proj_t, "core")
    summed_t = summed_directly(paired[:, :rows], "y")
    inverse = inverse_factor(paired, paired, rows // LANES)
    (partial_blocks,) = call(
        partial_kernel,
        columns // 2,
        [wide(rows), wide(rows), short, square],
        [((count // 2, ranks, LANES), F32, blocks(ranks))],
        [pltpu.VMEM((ranks, rows), F32)],
        flops=flops // 2,
        traffic=size // 2,
    )(high_half, low_half, summed_t, inverse)
    factor = both_halves(over_chips(partial_blocks))
    proj_t, gram = call(
        proj_kernel,
        columns,
        [blocks(ranks), wide(rows), wide(rows)],
        [((ranks, rows), F32, short), ((ranks, ranks), F32, square)],
        flops=flops,
        traffic=size,
    )(factor, high, low)
    paired = summed_directly(proj_t, "core")
    summed_t = summed_directly(paired, "y")
    inverse = inverse_factor(gram, paired)
    new_error, factor_rows = call(
        error_kernel,
        columns,
        [wide(rows), wide(rows), blocks(ranks), short, square],
        [
            ((1, rows, columns), F32, replica(rows)),
            ((3 * ranks, columns), BF16, wide(3 * ranks)),
        ],
        [pltpu.VMEM((rows, 3 * ranks), BF16)],
        flops=flops,
        traffic=2 * size,
    )(high, low, factor, proj_t, inverse)
    new_momentum, new_weights, basis_t = call(
        step_kernel,
        columns,
        [wide(3 * ranks), wide(rows), wide(rows), short, square],
        [
            ((rows, columns), F32, wide(rows)),
            ((rows, columns), BF16, wide(rows)),
            ((ranks, rows), F32, short),
        ],
        [pltpu.VMEM((rows, 3 * ranks), BF16)],
        flops=flops,
        traffic=3 * size,
    )(factor_rows, momentum, weights, summed_t, inverse)
    return new_error, new_momentum, new_weights, basis_t.T


def solution(mesh):
    grid = Mesh(mesh.devices.reshape(4, 2, 4, 8), ("y", "core", "x", "z"))
    island, shard = ("y", "core"), ("x", "z")
    in_specs = (
        P(island, shard, None),
        P(island, shard, None),
        P(shard, None),
        P(shard, None),
        P(shard, None),
    )
    out_specs = (P(island, shard, None), P(shard, None), P(shard, None), P(shard, None))
    return jax.shard_map(
        on_device, mesh=grid, in_specs=in_specs, out_specs=out_specs, check_vma=False
    )
```

```python
import functools

import jax
import jax.numpy as jnp
from jax import lax
from jax.experimental import pallas as pl
from jax.experimental.pallas import tpu as pltpu
from jax.sharding import Mesh, PartitionSpec as P

HIGHEST = lax.Precision.HIGHEST
F32, BF16 = jnp.float32, jnp.bfloat16
outer_beta = 0.9
outer_rate = 0.7
SIBLING = [(0, 1), (1, 0)]
LANES = 128
WIDE = 1024
PER = WIDE // LANES
CHUNK = 512


def halves(value):
    high = value.astype(BF16)
    return high, (value - high.astype(F32)).astype(BF16)


def dot(a, b, dims=((1,), (0,)), precision=None):
    return lax.dot_general(a, b, (dims, ((), ())), precision=precision, preferred_element_type=F32)


def joined(blocks_ref):
    return jnp.concatenate([blocks_ref[j] for j in range(PER)], axis=1)


def chunk_of(blocks_ref, c):
    per = CHUNK // LANES
    return jnp.concatenate([blocks_ref[c * per + j] for j in range(per)], axis=1)


def put_blocks(out_ref, value):
    for j in range(PER):
        out_ref[j] = value[:, j * LANES : (j + 1) * LANES]


def rank_product(basis_t, high, low):
    basis_high, basis_low = halves(basis_t)
    ranks = basis_t.shape[0]
    both = dot(jnp.concatenate([basis_high, basis_low], axis=0), high)
    return both[:ranks] + both[ranks:] + dot(basis_high, low)


def stacked_columns(factor_t):
    high, low = halves(factor_t.T)
    return jnp.concatenate([high, low, high], axis=1)


def column(side, place, columns):
    return pl.ds(pl.multiple_of(side * (columns // 2) + place * CHUNK, CHUNK), CHUNK)


def side_of(own):
    core = lax.axis_index("core")
    return core if own else 1 - core


def merge_kernel(own, grad_ref, error_ref, basis_ref, anchor_ref, merged_ref, partial_ref, grads, errors, basis, sems):
    columns = grad_ref.shape[2]
    count = columns // 2 // CHUNK
    side = side_of(own)
    start = pltpu.make_async_copy(basis_ref, basis, sems.at[2, count])
    start.start()
    copies = []
    for c in range(count):
        here = slice(c * CHUNK, (c + 1) * CHUNK)
        pair = [
            pltpu.make_async_copy(source.at[0, :, column(side, c, columns)], target.at[:, here], sems.at[i, c])
            for i, (source, target) in enumerate(((grad_ref, grads), (error_ref, errors)))
        ]
        for copy in pair:
            copy.start()
        copies.append(pair)
    leaving = []
    start.wait()
    for c, pair in enumerate(copies):
        here = slice(c * CHUNK, (c + 1) * CHUNK)
        for copy in pair:
            copy.wait()
        merged = grads[:, here] + errors[:, here]
        grads[:, here] = merged
        copy = pltpu.make_async_copy(grads.at[:, here], merged_ref.at[:, here], sems.at[2, c])
        copy.start()
        leaving.append(copy)
        partial = rank_product(basis[...], *halves(merged))
        for j in range(CHUNK // LANES):
            partial_ref[c * (CHUNK // LANES) + j] = partial[:, j * LANES : (j + 1) * LANES]
    for copy in leaving:
        copy.wait()


def partial_kernel(high_ref, low_ref, summed_ref, inverse_ref, partial_ref, basis_ref):
    @pl.when(pl.program_id(0) == 0)
    def _():
        basis_ref[...] = dot(inverse_ref[...], summed_ref[...], precision=HIGHEST)

    put_blocks(partial_ref, rank_product(basis_ref[...], high_ref[...], low_ref[...]))


ACROSS = ((1,), (1,))


def added_projection(totals, factor, high, low):
    both, rest, gram = totals
    ranks = factor.shape[0]
    factor_high, factor_low = halves(factor)
    last = (factor - factor_high.astype(F32) - factor_low.astype(F32)).astype(BF16)
    parts = jnp.concatenate([factor_high, factor_low, last], axis=0)
    return (
        both + dot(parts[: 2 * ranks], high, ACROSS),
        rest + dot(factor_high, low, ACROSS),
        gram + dot(parts, parts, ACROSS),
    )


def no_totals(ranks, rows):
    return (
        jnp.zeros((2 * ranks, rows), F32),
        jnp.zeros((ranks, rows), F32),
        jnp.zeros((3 * ranks, 3 * ranks), F32),
    )


def closed(totals):
    both, rest, gram = totals
    ranks = rest.shape[0]
    gram = gram[:ranks] + (gram[ranks : 2 * ranks] + gram[2 * ranks :])
    gram = gram[:, :ranks] + (gram[:, ranks : 2 * ranks] + gram[:, 2 * ranks :])
    return both[:ranks] + both[ranks:] + rest, gram


def paired_kernel(factor_ref, kept_ref, arrived_ref, out_ref, high_out, low_out, arrived, sems):
    rows, columns = kept_ref.shape
    ranks = factor_ref.shape[1]
    copies = []
    for c in range(columns // CHUNK):
        here = slice(c * CHUNK, (c + 1) * CHUNK)
        copies.append(pltpu.make_async_copy(arrived_ref.at[:, here], arrived.at[:, here], sems.at[c]))
        copies[-1].start()
    totals = no_totals(ranks, rows)
    for c, copy in enumerate(copies):
        here = slice(c * CHUNK, (c + 1) * CHUNK)
        copy.wait()
        high, low = halves(kept_ref[:, here] + arrived[:, here])
        high_out[:, here] = high
        low_out[:, here] = low
        totals = added_projection(totals, chunk_of(factor_ref, c), high, low)
    proj, gram = closed(totals)
    out_ref[:, :rows] = proj
    out_ref[:, rows:] = jnp.concatenate([gram, jnp.zeros((ranks, LANES - ranks), F32)], axis=1)


def half_projection(factor_ref, merged_ref):
    rows, columns = merged_ref.shape
    totals = no_totals(factor_ref.shape[1], rows)
    for c in range(columns // CHUNK):
        high, low = halves(merged_ref[:, c * CHUNK : (c + 1) * CHUNK])
        totals = added_projection(totals, chunk_of(factor_ref, c), high, low)
    return closed(totals)


def near_kernel(factor_ref, merged_ref, away_ref, out_ref, gram_ref, brought_ref, sem):
    copy = pltpu.make_async_copy(away_ref, brought_ref, sem)
    copy.start()
    out_ref[...], gram_ref[...] = half_projection(factor_ref, merged_ref)
    copy.wait()


def far_kernel(factor_ref, merged_ref, given_ref, given_gram_ref, out_ref, gram_ref):
    proj, gram = half_projection(factor_ref, merged_ref)
    out_ref[...] = given_ref[...] + proj
    gram_ref[...] = given_gram_ref[...] + gram


def three_rows(value):
    high, low = halves(value)
    return jnp.concatenate([high, high, low], axis=0)


def finish_kernel(
    kept_ref, away_ref, near_ref, far_ref, momentum_ref, weights_ref, proj_ref, summed_ref, inverse_ref,
    error_ref, new_momentum_ref, new_weights_ref, basis_ref, left, errors, momenta, stepped, sems,
):
    rows, columns = momentum_ref.shape
    count = columns // 2 // CHUNK
    inverse = inverse_ref[...]
    basis = dot(inverse, summed_ref[...], precision=HIGHEST)
    basis_ref[...] = basis
    left[:rows] = stacked_columns(dot(inverse, proj_ref[...], precision=HIGHEST))
    left[rows:] = stacked_columns(basis * 0.125)
    high, low = halves(inverse)
    turn = jnp.concatenate([high, low, high], axis=1)
    leaving = []
    for c in range(2 * count):
        here = slice(c * CHUNK, (c + 1) * CHUNK)
        own, place = c < count, c % count
        there = column(side_of(own), place, columns)
        factor_rows = three_rows(dot(turn, three_rows(chunk_of(near_ref if own else far_ref, place))))
        merged = (kept_ref if own else away_ref)[:, place * CHUNK : (place + 1) * CHUNK]
        errors[:, here] = merged - dot(left[:rows], factor_rows)
        update = dot(left[rows:], factor_rows)
        new_momentum = outer_beta * momentum_ref[:, there] + update
        momenta[:, here] = new_momentum
        step = outer_rate * (update + outer_beta * new_momentum)
        stepped[:, here] = (weights_ref[:, there].astype(F32) - step).astype(BF16)
        pairs = ((errors, error_ref.at[0]), (momenta, new_momentum_ref), (stepped, new_weights_ref))
        for i, (source, target) in enumerate(pairs):
            copy = pltpu.make_async_copy(source.at[:, here], target.at[:, there], sems.at[i, c])
            copy.start()
            leaving.append(copy)
    for copy in leaving:
        copy.wait()


def wide(rows):
    return pl.BlockSpec((rows, WIDE), lambda i: (0, i))


def whole(*shape):
    return pl.BlockSpec(shape, lambda i: (0,) * len(shape))


def blocks(ranks):
    return pl.BlockSpec((PER, ranks, LANES), lambda i: (i, 0, 0))


def call(kernel, columns, in_specs, outs, scratch=(), flops=0, traffic=0, limit=24):
    shapes = [jax.ShapeDtypeStruct(shape, kind) for shape, kind, _ in outs]
    specs = [spec for _, _, spec in outs]
    return pl.pallas_call(
        kernel,
        grid=(columns // WIDE,),
        in_specs=in_specs,
        out_shape=shapes,
        out_specs=specs,
        scratch_shapes=list(scratch),
        compiler_params=pltpu.CompilerParams(vmem_limit_bytes=limit * 2**20),
        cost_estimate=pl.CostEstimate(flops=flops, bytes_accessed=traffic, transcendentals=0),
    )


def around(axis, distance):
    size = lax.axis_size(axis)
    return [(i, (i + distance) % size) for i in range(size)]


def summed_directly(value, axis):
    size = lax.axis_size(axis)
    arrived = [lax.ppermute(value, axis, around(axis, d)) for d in range(1, size)]
    total = value
    for other in arrived:
        total = total + other
    return total


def to_everyone(piece, axes):
    size = lax.axis_size(axes)
    copies = jnp.broadcast_to(piece[None], (size, *piece.shape))
    return lax.all_to_all(copies, axes, 0, 0, tiled=True)


def over_chips(pieces):
    piece = lax.all_to_all(pieces, ("y", "x"), 0, 0, tiled=True).sum(axis=0)
    piece = to_everyone(piece, "z").sum(axis=0)
    return to_everyone(piece, ("y", "x"))


def spread(tile, column):
    return jnp.broadcast_to(tile[:, column : column + 1], tile.shape)


def inverse_kernel(gram_ref, anchor_ref, out_ref):
    ranks = out_ref.shape[0]
    gram = gram_ref[:, :ranks]
    row = lax.broadcasted_iota(jnp.int32, (ranks, ranks), 0)
    diagonal = row == lax.broadcasted_iota(jnp.int32, (ranks, ranks), 1)
    kept = jnp.where(diagonal, gram, 0.0)
    across = lax.rsqrt(jnp.sum(kept, axis=0, keepdims=True))
    down = lax.rsqrt(jnp.sum(kept, axis=1, keepdims=True))
    work = jnp.concatenate([gram * down * across, jnp.where(diagonal, across, 0.0)], axis=1)
    tiles = [work[8 * t : 8 * t + 8] for t in range(ranks // 8)]
    row = lax.broadcasted_iota(jnp.int32, (8, 2 * ranks), 0)
    out = []
    for j in range(0, ranks, 2):
        t, s = divmod(j, 8)
        left, right = spread(tiles[t], j), spread(tiles[t], j + 1)
        top, low = tiles[t][s : s + 1], tiles[t][s + 1 : s + 2]
        a, b, d = left[s : s + 1], left[s + 1 : s + 2], right[s + 1 : s + 2]
        det = a * d - b * b
        over = 1.0 / det
        rest = a * low - b * top
        first = (d * top - b * low) * over
        second = rest * over
        out.append(top * lax.rsqrt(a))
        out.append(rest * lax.rsqrt(a * det))
        for k in range(t, ranks // 8):
            if k > t:
                left, right = spread(tiles[k], j), spread(tiles[k], j + 1)
            elif s < 6:
                left = jnp.where(row > s + 1, left, 0.0)
                right = jnp.where(row > s + 1, right, 0.0)
            else:
                continue
            tiles[k] = tiles[k] - left * first - right * second
    out_ref[...] = jnp.concatenate(out, axis=0)[:, ranks:]


def inverse_factor(gram, anchor, block=0):
    ranks, width = gram.shape
    return pl.pallas_call(
        inverse_kernel,
        grid=(1,),
        in_specs=[
            pl.BlockSpec((ranks, min(width, LANES)), lambda i: (0, block)),
            pl.BlockSpec(memory_space=pl.ANY),
        ],
        out_specs=pl.BlockSpec((ranks, ranks), lambda i: (0, 0)),
        out_shape=jax.ShapeDtypeStruct((ranks, ranks), F32),
        compiler_params=pltpu.CompilerParams(vmem_limit_bytes=8 * 2**20),
        cost_estimate=pl.CostEstimate(flops=2 * 10**9, bytes_accessed=2**20, transcendentals=0),
    )(gram, anchor)


IN_VMEM = pl.BlockSpec(memory_space=pltpu.VMEM)
IN_HBM = pl.BlockSpec(memory_space=pltpu.HBM)


def in_hbm(array):
    return pltpu.with_memory_space_constraint(array, pltpu.HBM)


def flat_call(kernel, in_specs, out_shape, out_specs, scratch, flops, traffic):
    return pl.pallas_call(
        kernel,
        in_specs=in_specs,
        out_shape=out_shape,
        out_specs=out_specs,
        scratch_shapes=scratch,
        compiler_params=pltpu.CompilerParams(vmem_limit_bytes=24 * 2**20),
        cost_estimate=pl.CostEstimate(flops=flops, bytes_accessed=traffic, transcendentals=0),
    )


def merged_half(own, pseudo_grad, error_buffer, basis_t, anchor):
    _, rows, columns = pseudo_grad.shape
    ranks = basis_t.shape[0]
    half = columns // 2
    return flat_call(
        functools.partial(merge_kernel, own),
        [IN_HBM] * 3 + [pl.BlockSpec(memory_space=pl.ANY)],
        [pltpu.HBM((rows, half), F32), jax.ShapeDtypeStruct((half // LANES, ranks, LANES), F32)],
        [IN_HBM, IN_VMEM],
        [
            pltpu.VMEM((rows, half), F32),
            pltpu.VMEM((rows, half), F32),
            pltpu.VMEM((ranks, rows), F32),
            pltpu.SemaphoreType.DMA((3, half // CHUNK + 1)),
        ],
        6 * rows * half * ranks,
        12 * rows * half,
    )(in_hbm(pseudo_grad), in_hbm(error_buffer), in_hbm(basis_t), anchor)


def paired_product(factor, kept, arrived):
    _, ranks, _ = factor.shape
    rows, half = kept.shape
    share = jax.ShapeDtypeStruct((rows, half), BF16)
    return flat_call(
        paired_kernel,
        [IN_VMEM, IN_VMEM, IN_HBM],
        [jax.ShapeDtypeStruct((ranks, rows + LANES), F32), share, share],
        [IN_VMEM] * 3,
        [pltpu.VMEM((rows, half), F32), pltpu.SemaphoreType.DMA((half // CHUNK,))],
        6 * rows * half * ranks,
        12 * rows * half,
    )(factor, kept, in_hbm(arrived))


def near_product(factor, kept, away):
    _, ranks, _ = factor.shape
    rows, half = kept.shape
    return flat_call(
        near_kernel,
        [IN_VMEM, IN_VMEM, IN_HBM],
        [
            jax.ShapeDtypeStruct((ranks, rows), F32),
            jax.ShapeDtypeStruct((ranks, ranks), F32),
            jax.ShapeDtypeStruct((rows, half), F32),
        ],
        [IN_VMEM] * 3,
        [pltpu.SemaphoreType.DMA],
        6 * rows * half * ranks,
        8 * rows * half,
    )(factor, kept, in_hbm(away))


def far_product(factor, merged, proj_t, gram):
    _, ranks, _ = factor.shape
    rows, half = merged.shape
    return flat_call(
        far_kernel,
        [IN_VMEM] * 4,
        [jax.ShapeDtypeStruct((ranks, rows), F32), jax.ShapeDtypeStruct((ranks, ranks), F32)],
        [IN_VMEM] * 2,
        [],
        6 * rows * half * ranks,
        4 * rows * half,
    )(factor, merged, proj_t, gram)


def on_device(pseudo_grad, error_buffer, momentum, weights, warm_basis):
    _, rows, columns = pseudo_grad.shape
    ranks = warm_basis.shape[1]
    count = columns // LANES
    flops = 6 * rows * columns * ranks
    size = 4 * rows * columns
    short = whole(ranks, rows)
    square = whole(ranks, ranks)
    basis_t = warm_basis.T

    away, given = merged_half(False, pseudo_grad, error_buffer, basis_t, basis_t)
    kept, share = merged_half(True, pseudo_grad, error_buffer, basis_t, given)
    share = share + lax.ppermute(given, "core", SIBLING)
    share, leaving = lax.optimization_barrier((share, away))
    arrived = lax.ppermute(leaving, "core", SIBLING)
    proj_t, high_half, low_half = paired_product(over_chips(share), kept, arrived)
    paired = summed_directly(proj_t, "core")
    summed_t = summed_directly(paired[:, :rows], "y")
    inverse = inverse_factor(paired, paired, rows // LANES)
    (partial_blocks,) = call(
        partial_kernel,
        columns // 2,
        [wide(rows), wide(rows), short, square],
        [((count // 2, ranks, LANES), F32, blocks(ranks))],
        [pltpu.VMEM((ranks, rows), F32)],
        flops=flops // 2,
        traffic=size // 2,
    )(high_half, low_half, summed_t, inverse)
    near = over_chips(partial_blocks)
    far = lax.ppermute(near, "core", SIBLING)
    proj_t, gram, away = near_product(near, kept, away)
    proj_t, gram = far_product(far, away, proj_t, gram)
    paired = summed_directly(proj_t, "core")
    summed_t = summed_directly(paired, "y")
    inverse = inverse_factor(gram, paired)
    new_error, new_momentum, new_weights, basis_t = flat_call(
        finish_kernel,
        [IN_VMEM] * 9,
        [
            pltpu.HBM((1, rows, columns), F32),
            pltpu.HBM((rows, columns), F32),
            pltpu.HBM((rows, columns), BF16),
            jax.ShapeDtypeStruct((ranks, rows), F32),
        ],
        [IN_HBM] * 3 + [IN_VMEM],
        [
            pltpu.VMEM((2 * rows, 3 * ranks), BF16),
            pltpu.VMEM((rows, columns), F32),
            pltpu.VMEM((rows, columns), F32),
            pltpu.VMEM((rows, columns), BF16),
            pltpu.SemaphoreType.DMA((3, columns // CHUNK)),
        ],
        2 * flops,
        5 * size,
    )(kept, away, near, far, momentum, weights, proj_t, summed_t, inverse)
    return new_error, new_momentum, new_weights, basis_t.T


def solution(mesh):
    grid = Mesh(mesh.devices.reshape(4, 2, 4, 8), ("y", "core", "x", "z"))
    island, shard = ("y", "core"), ("x", "z")
    in_specs = (
        P(island, shard, None),
        P(island, shard, None),
        P(shard, None),
        P(shard, None),
        P(shard, None),
    )
    out_specs = (P(island, shard, None), P(shard, None), P(shard, None), P(shard, None))
    return jax.shard_map(
        on_device, mesh=grid, in_specs=in_specs, out_specs=out_specs, check_vma=False
    )
```

```python
import functools

import jax
import jax.numpy as jnp
from jax import lax
from jax.experimental import pallas as pl
from jax.experimental.pallas import tpu as pltpu
from jax.sharding import Mesh, PartitionSpec as P

HIGHEST = lax.Precision.HIGHEST
F32, BF16 = jnp.float32, jnp.bfloat16
outer_beta = 0.9
outer_rate = 0.7
SIBLING = [(0, 1), (1, 0)]
LANES = 128
WIDE = 1024
PER = WIDE // LANES
CHUNK = 512


def halves(value):
    high = value.astype(BF16)
    return high, (value - high.astype(F32)).astype(BF16)


def dot(a, b, dims=((1,), (0,)), precision=None):
    return lax.dot_general(a, b, (dims, ((), ())), precision=precision, preferred_element_type=F32)


def joined(blocks_ref):
    return jnp.concatenate([blocks_ref[j] for j in range(PER)], axis=1)


def chunk_of(blocks_ref, c):
    per = CHUNK // LANES
    return jnp.concatenate([blocks_ref[c * per + j] for j in range(per)], axis=1)


def put_blocks(out_ref, value):
    for j in range(PER):
        out_ref[j] = value[:, j * LANES : (j + 1) * LANES]


def rank_product(basis_t, high, low):
    basis_high, basis_low = halves(basis_t)
    ranks = basis_t.shape[0]
    both = dot(jnp.concatenate([basis_high, basis_low], axis=0), high)
    return both[:ranks] + both[ranks:] + dot(basis_high, low)


def stacked_columns(factor_t):
    high, low = halves(factor_t.T)
    return jnp.concatenate([high, low, high], axis=1)


def column(side, place, columns):
    return pl.ds(pl.multiple_of(side * (columns // 2) + place * CHUNK, CHUNK), CHUNK)


def side_of(own):
    core = lax.axis_index("core")
    return core if own else 1 - core


def merge_kernel(own, grad_ref, error_ref, basis_ref, anchor_ref, merged_ref, partial_ref, grads, errors, basis, sems):
    columns = grad_ref.shape[2]
    count = columns // 2 // CHUNK
    side = side_of(own)
    start = pltpu.make_async_copy(basis_ref, basis, sems.at[2, count])
    start.start()
    copies = []
    for c in range(count):
        here = slice(c * CHUNK, (c + 1) * CHUNK)
        pair = [
            pltpu.make_async_copy(source.at[0, :, column(side, c, columns)], target.at[:, here], sems.at[i, c])
            for i, (source, target) in enumerate(((grad_ref, grads), (error_ref, errors)))
        ]
        for copy in pair:
            copy.start()
        copies.append(pair)
    leaving = []
    start.wait()
    for c, pair in enumerate(copies):
        here = slice(c * CHUNK, (c + 1) * CHUNK)
        for copy in pair:
            copy.wait()
        merged = grads[:, here] + errors[:, here]
        if own:
            merged_ref[:, here] = merged
        else:
            grads[:, here] = merged
            copy = pltpu.make_async_copy(grads.at[:, here], merged_ref.at[:, here], sems.at[2, c])
            copy.start()
            leaving.append(copy)
        partial = rank_product(basis[...], *halves(merged))
        for j in range(CHUNK // LANES):
            partial_ref[c * (CHUNK // LANES) + j] = partial[:, j * LANES : (j + 1) * LANES]
    for copy in leaving:
        copy.wait()


def partial_kernel(high_ref, low_ref, summed_ref, inverse_ref, partial_ref, basis_ref):
    @pl.when(pl.program_id(0) == 0)
    def _():
        basis_ref[...] = dot(inverse_ref[...], summed_ref[...], precision=HIGHEST)

    put_blocks(partial_ref, rank_product(basis_ref[...], high_ref[...], low_ref[...]))


ACROSS = ((1,), (1,))


def added_projection(totals, factor, high, low):
    both, rest, gram = totals
    ranks = factor.shape[0]
    factor_high, factor_low = halves(factor)
    last = (factor - factor_high.astype(F32) - factor_low.astype(F32)).astype(BF16)
    parts = jnp.concatenate([factor_high, factor_low, last], axis=0)
    return (
        both + dot(parts[: 2 * ranks], high, ACROSS),
        rest + dot(factor_high, low, ACROSS),
        gram + dot(parts, parts, ACROSS),
    )


def no_totals(ranks, rows):
    return (
        jnp.zeros((2 * ranks, rows), F32),
        jnp.zeros((ranks, rows), F32),
        jnp.zeros((3 * ranks, 3 * ranks), F32),
    )


def closed(totals):
    both, rest, gram = totals
    ranks = rest.shape[0]
    gram = gram[:ranks] + (gram[ranks : 2 * ranks] + gram[2 * ranks :])
    gram = gram[:, :ranks] + (gram[:, ranks : 2 * ranks] + gram[:, 2 * ranks :])
    return both[:ranks] + both[ranks:] + rest, gram


def paired_kernel(factor_ref, kept_ref, arrived_ref, out_ref, high_out, low_out, arrived, sems):
    rows, columns = kept_ref.shape
    ranks = factor_ref.shape[1]
    copies = []
    for c in range(columns // CHUNK):
        here = slice(c * CHUNK, (c + 1) * CHUNK)
        copies.append(pltpu.make_async_copy(arrived_ref.at[:, here], arrived.at[:, here], sems.at[c]))
        copies[-1].start()
    totals = no_totals(ranks, rows)
    for c, copy in enumerate(copies):
        here = slice(c * CHUNK, (c + 1) * CHUNK)
        copy.wait()
        high, low = halves(kept_ref[:, here] + arrived[:, here])
        high_out[:, here] = high
        low_out[:, here] = low
        totals = added_projection(totals, chunk_of(factor_ref, c), high, low)
    proj, gram = closed(totals)
    out_ref[:, :rows] = proj
    out_ref[:, rows:] = jnp.concatenate([gram, jnp.zeros((ranks, LANES - ranks), F32)], axis=1)


def half_projection(factor_ref, merged_ref):
    rows, columns = merged_ref.shape
    totals = no_totals(factor_ref.shape[1], rows)
    for c in range(columns // CHUNK):
        high, low = halves(merged_ref[:, c * CHUNK : (c + 1) * CHUNK])
        totals = added_projection(totals, chunk_of(factor_ref, c), high, low)
    return closed(totals)


def near_kernel(factor_ref, merged_ref, away_ref, out_ref, gram_ref, brought_ref, sem):
    copy = pltpu.make_async_copy(away_ref, brought_ref, sem)
    copy.start()
    out_ref[...], gram_ref[...] = half_projection(factor_ref, merged_ref)
    copy.wait()


def far_kernel(factor_ref, merged_ref, given_ref, given_gram_ref, out_ref, gram_ref):
    proj, gram = half_projection(factor_ref, merged_ref)
    out_ref[...] = given_ref[...] + proj
    gram_ref[...] = given_gram_ref[...] + gram


def three_rows(value):
    high, low = halves(value)
    return jnp.concatenate([high, high, low], axis=0)


def finish_kernel(
    kept_ref, away_ref, near_ref, far_ref, momentum_ref, weights_ref, proj_ref, summed_ref, inverse_ref,
    error_ref, new_momentum_ref, new_weights_ref, basis_ref, left, errors, momenta, stepped, sems,
):
    rows, columns = momentum_ref.shape
    count = columns // 2 // CHUNK
    inverse = inverse_ref[...]
    basis = dot(inverse, summed_ref[...], precision=HIGHEST)
    basis_ref[...] = basis
    left[:rows] = stacked_columns(dot(inverse, proj_ref[...], precision=HIGHEST))
    left[rows:] = stacked_columns(basis * 0.125)
    high, low = halves(inverse)
    turn = jnp.concatenate([high, low, high], axis=1)
    leaving = []
    for c in range(2 * count):
        here = slice(c * CHUNK, (c + 1) * CHUNK)
        own, place = c < count, c % count
        there = column(side_of(own), place, columns)
        factor_rows = three_rows(dot(turn, three_rows(chunk_of(near_ref if own else far_ref, place))))
        merged = (kept_ref if own else away_ref)[:, place * CHUNK : (place + 1) * CHUNK]
        errors[:, here] = merged - dot(left[:rows], factor_rows)
        update = dot(left[rows:], factor_rows)
        new_momentum = outer_beta * momentum_ref[:, there] + update
        momenta[:, here] = new_momentum
        step = outer_rate * (update + outer_beta * new_momentum)
        stepped[:, here] = (weights_ref[:, there].astype(F32) - step).astype(BF16)
        pairs = ((errors, error_ref.at[0]), (momenta, new_momentum_ref), (stepped, new_weights_ref))
        for i, (source, target) in enumerate(pairs):
            copy = pltpu.make_async_copy(source.at[:, here], target.at[:, there], sems.at[i, c])
            copy.start()
            leaving.append(copy)
    for copy in leaving:
        copy.wait()


def wide(rows):
    return pl.BlockSpec((rows, WIDE), lambda i: (0, i))


def whole(*shape):
    return pl.BlockSpec(shape, lambda i: (0,) * len(shape))


def blocks(ranks):
    return pl.BlockSpec((PER, ranks, LANES), lambda i: (i, 0, 0))


def call(kernel, columns, in_specs, outs, scratch=(), flops=0, traffic=0, limit=24):
    shapes = [jax.ShapeDtypeStruct(shape, kind) for shape, kind, _ in outs]
    specs = [spec for _, _, spec in outs]
    return pl.pallas_call(
        kernel,
        grid=(columns // WIDE,),
        in_specs=in_specs,
        out_shape=shapes,
        out_specs=specs,
        scratch_shapes=list(scratch),
        compiler_params=pltpu.CompilerParams(vmem_limit_bytes=limit * 2**20),
        cost_estimate=pl.CostEstimate(flops=flops, bytes_accessed=traffic, transcendentals=0),
    )


def around(axis, distance):
    size = lax.axis_size(axis)
    return [(i, (i + distance) % size) for i in range(size)]


def summed_directly(value, axis):
    size = lax.axis_size(axis)
    arrived = [lax.ppermute(value, axis, around(axis, d)) for d in range(1, size)]
    total = value
    for other in arrived:
        total = total + other
    return total


def to_everyone(piece, axes):
    size = lax.axis_size(axes)
    copies = jnp.broadcast_to(piece[None], (size, *piece.shape))
    return lax.all_to_all(copies, axes, 0, 0, tiled=True)


def over_chips(pieces):
    piece = lax.all_to_all(pieces, ("y", "x"), 0, 0, tiled=True).sum(axis=0)
    piece = to_everyone(piece, "z").sum(axis=0)
    return to_everyone(piece, ("y", "x"))


def spread(tile, column):
    return jnp.broadcast_to(tile[:, column : column + 1], tile.shape)


def inverse_kernel(gram_ref, anchor_ref, out_ref):
    ranks = out_ref.shape[0]
    gram = gram_ref[:, :ranks]
    row = lax.broadcasted_iota(jnp.int32, (ranks, ranks), 0)
    diagonal = row == lax.broadcasted_iota(jnp.int32, (ranks, ranks), 1)
    kept = jnp.where(diagonal, gram, 0.0)
    across = lax.rsqrt(jnp.sum(kept, axis=0, keepdims=True))
    down = lax.rsqrt(jnp.sum(kept, axis=1, keepdims=True))
    work = jnp.concatenate([gram * down * across, jnp.where(diagonal, across, 0.0)], axis=1)
    tiles = [work[8 * t : 8 * t + 8] for t in range(ranks // 8)]
    row = lax.broadcasted_iota(jnp.int32, (8, 2 * ranks), 0)
    out = []
    for j in range(0, ranks, 2):
        t, s = divmod(j, 8)
        left, right = spread(tiles[t], j), spread(tiles[t], j + 1)
        top, low = tiles[t][s : s + 1], tiles[t][s + 1 : s + 2]
        a, b, d = left[s : s + 1], left[s + 1 : s + 2], right[s + 1 : s + 2]
        det = a * d - b * b
        over = 1.0 / det
        rest = a * low - b * top
        first = (d * top - b * low) * over
        second = rest * over
        out.append(top * lax.rsqrt(a))
        out.append(rest * lax.rsqrt(a * det))
        for k in range(t, ranks // 8):
            if k > t:
                left, right = spread(tiles[k], j), spread(tiles[k], j + 1)
            elif s < 6:
                left = jnp.where(row > s + 1, left, 0.0)
                right = jnp.where(row > s + 1, right, 0.0)
            else:
                continue
            tiles[k] = tiles[k] - left * first - right * second
    out_ref[...] = jnp.concatenate(out, axis=0)[:, ranks:]


def inverse_factor(gram, anchor, block=0):
    ranks, width = gram.shape
    return pl.pallas_call(
        inverse_kernel,
        grid=(1,),
        in_specs=[
            pl.BlockSpec((ranks, min(width, LANES)), lambda i: (0, block)),
            pl.BlockSpec(memory_space=pl.ANY),
        ],
        out_specs=pl.BlockSpec((ranks, ranks), lambda i: (0, 0)),
        out_shape=jax.ShapeDtypeStruct((ranks, ranks), F32),
        compiler_params=pltpu.CompilerParams(vmem_limit_bytes=8 * 2**20),
        cost_estimate=pl.CostEstimate(flops=2 * 10**9, bytes_accessed=2**20, transcendentals=0),
    )(gram, anchor)


IN_VMEM = pl.BlockSpec(memory_space=pltpu.VMEM)
IN_HBM = pl.BlockSpec(memory_space=pltpu.HBM)


def in_hbm(array):
    return pltpu.with_memory_space_constraint(array, pltpu.HBM)


def flat_call(kernel, in_specs, out_shape, out_specs, scratch, flops, traffic):
    return pl.pallas_call(
        kernel,
        in_specs=in_specs,
        out_shape=out_shape,
        out_specs=out_specs,
        scratch_shapes=scratch,
        compiler_params=pltpu.CompilerParams(vmem_limit_bytes=24 * 2**20),
        cost_estimate=pl.CostEstimate(flops=flops, bytes_accessed=traffic, transcendentals=0),
    )


def merged_half(own, pseudo_grad, error_buffer, basis_t, anchor):
    _, rows, columns = pseudo_grad.shape
    ranks = basis_t.shape[0]
    half = columns // 2
    merged = jax.ShapeDtypeStruct((rows, half), F32) if own else pltpu.HBM((rows, half), F32)
    return flat_call(
        functools.partial(merge_kernel, own),
        [IN_HBM] * 3 + [pl.BlockSpec(memory_space=pl.ANY)],
        [merged, jax.ShapeDtypeStruct((half // LANES, ranks, LANES), F32)],
        [IN_VMEM if own else IN_HBM, IN_VMEM],
        [
            pltpu.VMEM((rows, half), F32),
            pltpu.VMEM((rows, half), F32),
            pltpu.VMEM((ranks, rows), F32),
            pltpu.SemaphoreType.DMA((3, half // CHUNK + 1)),
        ],
        6 * rows * half * ranks,
        12 * rows * half,
    )(in_hbm(pseudo_grad), in_hbm(error_buffer), in_hbm(basis_t), anchor)


def paired_product(factor, kept, arrived):
    _, ranks, _ = factor.shape
    rows, half = kept.shape
    share = jax.ShapeDtypeStruct((rows, half), BF16)
    return flat_call(
        paired_kernel,
        [IN_VMEM, IN_VMEM, IN_HBM],
        [jax.ShapeDtypeStruct((ranks, rows + LANES), F32), share, share],
        [IN_VMEM] * 3,
        [pltpu.VMEM((rows, half), F32), pltpu.SemaphoreType.DMA((half // CHUNK,))],
        6 * rows * half * ranks,
        12 * rows * half,
    )(factor, kept, in_hbm(arrived))


def near_product(factor, kept, away):
    _, ranks, _ = factor.shape
    rows, half = kept.shape
    return flat_call(
        near_kernel,
        [IN_VMEM, IN_VMEM, IN_HBM],
        [
            jax.ShapeDtypeStruct((ranks, rows), F32),
            jax.ShapeDtypeStruct((ranks, ranks), F32),
            jax.ShapeDtypeStruct((rows, half), F32),
        ],
        [IN_VMEM] * 3,
        [pltpu.SemaphoreType.DMA],
        6 * rows * half * ranks,
        8 * rows * half,
    )(factor, kept, in_hbm(away))


def far_product(factor, merged, proj_t, gram):
    _, ranks, _ = factor.shape
    rows, half = merged.shape
    return flat_call(
        far_kernel,
        [IN_VMEM] * 4,
        [jax.ShapeDtypeStruct((ranks, rows), F32), jax.ShapeDtypeStruct((ranks, ranks), F32)],
        [IN_VMEM] * 2,
        [],
        6 * rows * half * ranks,
        4 * rows * half,
    )(factor, merged, proj_t, gram)


def on_device(pseudo_grad, error_buffer, momentum, weights, warm_basis):
    _, rows, columns = pseudo_grad.shape
    ranks = warm_basis.shape[1]
    count = columns // LANES
    flops = 6 * rows * columns * ranks
    size = 4 * rows * columns
    short = whole(ranks, rows)
    square = whole(ranks, ranks)
    basis_t = warm_basis.T

    away, given = merged_half(False, pseudo_grad, error_buffer, basis_t, basis_t)
    kept, share = merged_half(True, pseudo_grad, error_buffer, basis_t, given)
    share = share + lax.ppermute(given, "core", SIBLING)
    share, leaving = lax.optimization_barrier((share, away))
    arrived = lax.ppermute(leaving, "core", SIBLING)
    proj_t, high_half, low_half = paired_product(over_chips(share), kept, arrived)
    paired = summed_directly(proj_t, "core")
    summed_t = summed_directly(paired[:, :rows], "y")
    inverse = inverse_factor(paired, paired, rows // LANES)
    (partial_blocks,) = call(
        partial_kernel,
        columns // 2,
        [wide(rows), wide(rows), short, square],
        [((count // 2, ranks, LANES), F32, blocks(ranks))],
        [pltpu.VMEM((ranks, rows), F32)],
        flops=flops // 2,
        traffic=size // 2,
    )(high_half, low_half, summed_t, inverse)
    near = over_chips(partial_blocks)
    far = lax.ppermute(near, "core", SIBLING)
    proj_t, gram, away = near_product(near, kept, away)
    proj_t, gram = far_product(far, away, proj_t, gram)
    paired = summed_directly(proj_t, "core")
    summed_t = summed_directly(paired, "y")
    inverse = inverse_factor(gram, paired)
    new_error, new_momentum, new_weights, basis_t = flat_call(
        finish_kernel,
        [IN_VMEM] * 9,
        [
            pltpu.HBM((1, rows, columns), F32),
            pltpu.HBM((rows, columns), F32),
            pltpu.HBM((rows, columns), BF16),
            jax.ShapeDtypeStruct((ranks, rows), F32),
        ],
        [IN_HBM] * 3 + [IN_VMEM],
        [
            pltpu.VMEM((2 * rows, 3 * ranks), BF16),
            pltpu.VMEM((rows, columns), F32),
            pltpu.VMEM((rows, columns), F32),
            pltpu.VMEM((rows, columns), BF16),
            pltpu.SemaphoreType.DMA((3, columns // CHUNK)),
        ],
        2 * flops,
        5 * size,
    )(kept, away, near, far, momentum, weights, proj_t, summed_t, inverse)
    return new_error, new_momentum, new_weights, basis_t.T


def solution(mesh):
    grid = Mesh(mesh.devices.reshape(4, 2, 4, 8), ("y", "core", "x", "z"))
    island, shard = ("y", "core"), ("x", "z")
    in_specs = (
        P(island, shard, None),
        P(island, shard, None),
        P(shard, None),
        P(shard, None),
        P(shard, None),
    )
    out_specs = (P(island, shard, None), P(shard, None), P(shard, None), P(shard, None))
    return jax.shard_map(
        on_device, mesh=grid, in_specs=in_specs, out_specs=out_specs, check_vma=False
    )
```

```python
import functools

import jax
import jax.numpy as jnp
from jax import lax
from jax.experimental import pallas as pl
from jax.experimental.pallas import tpu as pltpu
from jax.sharding import Mesh, PartitionSpec as P

HIGHEST = lax.Precision.HIGHEST
F32, BF16 = jnp.float32, jnp.bfloat16
outer_beta = 0.9
outer_rate = 0.7
SIBLING = [(0, 1), (1, 0)]
LANES = 128
WIDE = 1024
PER = WIDE // LANES
CHUNK = 512


def halves(value):
    high = value.astype(BF16)
    return high, (value - high.astype(F32)).astype(BF16)


def dot(a, b, dims=((1,), (0,)), precision=None):
    return lax.dot_general(a, b, (dims, ((), ())), precision=precision, preferred_element_type=F32)


def joined(blocks_ref):
    return jnp.concatenate([blocks_ref[j] for j in range(PER)], axis=1)


def chunk_of(blocks_ref, c):
    per = CHUNK // LANES
    return jnp.concatenate([blocks_ref[c * per + j] for j in range(per)], axis=1)


def put_blocks(out_ref, value):
    for j in range(PER):
        out_ref[j] = value[:, j * LANES : (j + 1) * LANES]


def rank_product(basis_t, high, low):
    basis_high, basis_low = halves(basis_t)
    ranks = basis_t.shape[0]
    both = dot(jnp.concatenate([basis_high, basis_low], axis=0), high)
    return both[:ranks] + both[ranks:] + dot(basis_high, low)


def stacked_columns(factor_t):
    high, low = halves(factor_t.T)
    return jnp.concatenate([high, low, high], axis=1)


def column(side, place, columns):
    return pl.ds(pl.multiple_of(side * (columns // 2) + place * CHUNK, CHUNK), CHUNK)


def side_of(own):
    core = lax.axis_index("core")
    return core if own else 1 - core


def merge_kernel(own, grad_ref, error_ref, basis_ref, other_ref, merged_ref, partial_ref, *refs):
    columns = grad_ref.shape[2]
    count = columns // 2 // CHUNK
    side = side_of(own)
    grads, errors, basis, sems = refs[-4:]
    start = pltpu.make_async_copy(basis_ref, basis, sems.at[2, count])
    start.start()
    if own:
        leaving = pltpu.make_async_copy(other_ref, refs[0], sems.at[2, 0])
        leaving.start()
    copies = []
    for c in range(count):
        here = slice(c * CHUNK, (c + 1) * CHUNK)
        pair = [
            pltpu.make_async_copy(source.at[0, :, column(side, c, columns)], target.at[:, here], sems.at[i, c])
            for i, (source, target) in enumerate(((grad_ref, grads), (error_ref, errors)))
        ]
        for copy in pair:
            copy.start()
        copies.append(pair)
    start.wait()
    for c, pair in enumerate(copies):
        here = slice(c * CHUNK, (c + 1) * CHUNK)
        for copy in pair:
            copy.wait()
        merged = grads[:, here] + errors[:, here]
        merged_ref[:, here] = merged
        partial = rank_product(basis[...], *halves(merged))
        for j in range(CHUNK // LANES):
            partial_ref[c * (CHUNK // LANES) + j] = partial[:, j * LANES : (j + 1) * LANES]
    if own:
        leaving.wait()


def partial_kernel(high_ref, low_ref, summed_ref, inverse_ref, partial_ref, basis_ref):
    @pl.when(pl.program_id(0) == 0)
    def _():
        basis_ref[...] = dot(inverse_ref[...], summed_ref[...], precision=HIGHEST)

    put_blocks(partial_ref, rank_product(basis_ref[...], high_ref[...], low_ref[...]))


ACROSS = ((1,), (1,))


def added_projection(totals, factor, high, low):
    both, rest, gram = totals
    ranks = factor.shape[0]
    factor_high, factor_low = halves(factor)
    last = (factor - factor_high.astype(F32) - factor_low.astype(F32)).astype(BF16)
    parts = jnp.concatenate([factor_high, factor_low, last], axis=0)
    return (
        both + dot(parts[: 2 * ranks], high, ACROSS),
        rest + dot(factor_high, low, ACROSS),
        gram + dot(parts, parts, ACROSS),
    )


def no_totals(ranks, rows):
    return (
        jnp.zeros((2 * ranks, rows), F32),
        jnp.zeros((ranks, rows), F32),
        jnp.zeros((3 * ranks, 3 * ranks), F32),
    )


def closed(totals):
    both, rest, gram = totals
    ranks = rest.shape[0]
    gram = gram[:ranks] + (gram[ranks : 2 * ranks] + gram[2 * ranks :])
    gram = gram[:, :ranks] + (gram[:, ranks : 2 * ranks] + gram[:, 2 * ranks :])
    return both[:ranks] + both[ranks:] + rest, gram


def paired_kernel(factor_ref, kept_ref, arrived_ref, out_ref, high_out, low_out, arrived, sems):
    rows, columns = kept_ref.shape
    ranks = factor_ref.shape[1]
    copies = []
    for c in range(columns // CHUNK):
        here = slice(c * CHUNK, (c + 1) * CHUNK)
        copies.append(pltpu.make_async_copy(arrived_ref.at[:, here], arrived.at[:, here], sems.at[c]))
        copies[-1].start()
    totals = no_totals(ranks, rows)
    for c, copy in enumerate(copies):
        here = slice(c * CHUNK, (c + 1) * CHUNK)
        copy.wait()
        high, low = halves(kept_ref[:, here] + arrived[:, here])
        high_out[:, here] = high
        low_out[:, here] = low
        totals = added_projection(totals, chunk_of(factor_ref, c), high, low)
    proj, gram = closed(totals)
    out_ref[:, :rows] = proj
    out_ref[:, rows:] = jnp.concatenate([gram, jnp.zeros((ranks, LANES - ranks), F32)], axis=1)


def half_projection(factor_ref, merged_ref):
    rows, columns = merged_ref.shape
    totals = no_totals(factor_ref.shape[1], rows)
    for c in range(columns // CHUNK):
        high, low = halves(merged_ref[:, c * CHUNK : (c + 1) * CHUNK])
        totals = added_projection(totals, chunk_of(factor_ref, c), high, low)
    return closed(totals)


def near_kernel(factor_ref, merged_ref, away_ref, out_ref, gram_ref, brought_ref, sem):
    copy = pltpu.make_async_copy(away_ref, brought_ref, sem)
    copy.start()
    out_ref[...], gram_ref[...] = half_projection(factor_ref, merged_ref)
    copy.wait()


def far_kernel(factor_ref, merged_ref, given_ref, given_gram_ref, out_ref, gram_ref):
    proj, gram = half_projection(factor_ref, merged_ref)
    out_ref[...] = given_ref[...] + proj
    gram_ref[...] = given_gram_ref[...] + gram


def three_rows(value):
    high, low = halves(value)
    return jnp.concatenate([high, high, low], axis=0)


def finish_kernel(
    kept_ref, away_ref, near_ref, far_ref, momentum_ref, weights_ref, proj_ref, summed_ref, inverse_ref,
    error_ref, new_momentum_ref, new_weights_ref, basis_ref, left, errors, momenta, stepped, sems,
):
    rows, columns = momentum_ref.shape
    count = columns // 2 // CHUNK
    inverse = inverse_ref[...]
    basis = dot(inverse, summed_ref[...], precision=HIGHEST)
    basis_ref[...] = basis
    left[:rows] = stacked_columns(dot(inverse, proj_ref[...], precision=HIGHEST))
    left[rows:] = stacked_columns(basis * 0.125)
    high, low = halves(inverse)
    turn = jnp.concatenate([high, low, high], axis=1)
    leaving = []
    for c in range(2 * count):
        here = slice(c * CHUNK, (c + 1) * CHUNK)
        own, place = c < count, c % count
        there = column(side_of(own), place, columns)
        factor_rows = three_rows(dot(turn, three_rows(chunk_of(near_ref if own else far_ref, place))))
        merged = (kept_ref if own else away_ref)[:, place * CHUNK : (place + 1) * CHUNK]
        errors[:, here] = merged - dot(left[:rows], factor_rows)
        update = dot(left[rows:], factor_rows)
        new_momentum = outer_beta * momentum_ref[:, there] + update
        momenta[:, here] = new_momentum
        step = outer_rate * (update + outer_beta * new_momentum)
        stepped[:, here] = (weights_ref[:, there].astype(F32) - step).astype(BF16)
        pairs = ((errors, error_ref.at[0]), (momenta, new_momentum_ref), (stepped, new_weights_ref))
        for i, (source, target) in enumerate(pairs):
            copy = pltpu.make_async_copy(source.at[:, here], target.at[:, there], sems.at[i, c])
            copy.start()
            leaving.append(copy)
    for copy in leaving:
        copy.wait()


def wide(rows):
    return pl.BlockSpec((rows, WIDE), lambda i: (0, i))


def whole(*shape):
    return pl.BlockSpec(shape, lambda i: (0,) * len(shape))


def blocks(ranks):
    return pl.BlockSpec((PER, ranks, LANES), lambda i: (i, 0, 0))


def call(kernel, columns, in_specs, outs, scratch=(), flops=0, traffic=0, limit=24):
    shapes = [jax.ShapeDtypeStruct(shape, kind) for shape, kind, _ in outs]
    specs = [spec for _, _, spec in outs]
    return pl.pallas_call(
        kernel,
        grid=(columns // WIDE,),
        in_specs=in_specs,
        out_shape=shapes,
        out_specs=specs,
        scratch_shapes=list(scratch),
        compiler_params=pltpu.CompilerParams(vmem_limit_bytes=limit * 2**20),
        cost_estimate=pl.CostEstimate(flops=flops, bytes_accessed=traffic, transcendentals=0),
    )


def around(axis, distance):
    size = lax.axis_size(axis)
    return [(i, (i + distance) % size) for i in range(size)]


def summed_directly(value, axis):
    size = lax.axis_size(axis)
    arrived = [lax.ppermute(value, axis, around(axis, d)) for d in range(1, size)]
    total = value
    for other in arrived:
        total = total + other
    return total


def to_everyone(piece, axes):
    size = lax.axis_size(axes)
    copies = jnp.broadcast_to(piece[None], (size, *piece.shape))
    return lax.all_to_all(copies, axes, 0, 0, tiled=True)


def over_chips(pieces):
    piece = lax.all_to_all(pieces, ("y", "x"), 0, 0, tiled=True).sum(axis=0)
    piece = to_everyone(piece, "z").sum(axis=0)
    return to_everyone(piece, ("y", "x"))


def spread(tile, column):
    return jnp.broadcast_to(tile[:, column : column + 1], tile.shape)


def inverse_kernel(gram_ref, anchor_ref, out_ref):
    ranks = out_ref.shape[0]
    gram = gram_ref[:, :ranks]
    row = lax.broadcasted_iota(jnp.int32, (ranks, ranks), 0)
    diagonal = row == lax.broadcasted_iota(jnp.int32, (ranks, ranks), 1)
    kept = jnp.where(diagonal, gram, 0.0)
    across = lax.rsqrt(jnp.sum(kept, axis=0, keepdims=True))
    down = lax.rsqrt(jnp.sum(kept, axis=1, keepdims=True))
    work = jnp.concatenate([gram * down * across, jnp.where(diagonal, across, 0.0)], axis=1)
    tiles = [work[8 * t : 8 * t + 8] for t in range(ranks // 8)]
    row = lax.broadcasted_iota(jnp.int32, (8, 2 * ranks), 0)
    out = []
    for j in range(0, ranks, 2):
        t, s = divmod(j, 8)
        left, right = spread(tiles[t], j), spread(tiles[t], j + 1)
        top, low = tiles[t][s : s + 1], tiles[t][s + 1 : s + 2]
        a, b, d = left[s : s + 1], left[s + 1 : s + 2], right[s + 1 : s + 2]
        det = a * d - b * b
        over = 1.0 / det
        rest = a * low - b * top
        first = (d * top - b * low) * over
        second = rest * over
        out.append(top * lax.rsqrt(a))
        out.append(rest * lax.rsqrt(a * det))
        for k in range(t, ranks // 8):
            if k > t:
                left, right = spread(tiles[k], j), spread(tiles[k], j + 1)
            elif s < 6:
                left = jnp.where(row > s + 1, left, 0.0)
                right = jnp.where(row > s + 1, right, 0.0)
            else:
                continue
            tiles[k] = tiles[k] - left * first - right * second
    out_ref[...] = jnp.concatenate(out, axis=0)[:, ranks:]


def inverse_factor(gram, anchor, block=0):
    ranks, width = gram.shape
    return pl.pallas_call(
        inverse_kernel,
        grid=(1,),
        in_specs=[
            pl.BlockSpec((ranks, min(width, LANES)), lambda i: (0, block)),
            pl.BlockSpec(memory_space=pl.ANY),
        ],
        out_specs=pl.BlockSpec((ranks, ranks), lambda i: (0, 0)),
        out_shape=jax.ShapeDtypeStruct((ranks, ranks), F32),
        compiler_params=pltpu.CompilerParams(vmem_limit_bytes=8 * 2**20),
        cost_estimate=pl.CostEstimate(flops=2 * 10**9, bytes_accessed=2**20, transcendentals=0),
    )(gram, anchor)


IN_VMEM = pl.BlockSpec(memory_space=pltpu.VMEM)
IN_HBM = pl.BlockSpec(memory_space=pltpu.HBM)


def in_hbm(array):
    return pltpu.with_memory_space_constraint(array, pltpu.HBM)


def flat_call(kernel, in_specs, out_shape, out_specs, scratch, flops, traffic):
    return pl.pallas_call(
        kernel,
        in_specs=in_specs,
        out_shape=out_shape,
        out_specs=out_specs,
        scratch_shapes=scratch,
        compiler_params=pltpu.CompilerParams(vmem_limit_bytes=24 * 2**20),
        cost_estimate=pl.CostEstimate(flops=flops, bytes_accessed=traffic, transcendentals=0),
    )


def merged_half(own, pseudo_grad, error_buffer, basis_t, anchor):
    _, rows, columns = pseudo_grad.shape
    ranks = basis_t.shape[0]
    half = columns // 2
    return flat_call(
        functools.partial(merge_kernel, own),
        [IN_HBM] * 3 + [IN_VMEM if own else pl.BlockSpec(memory_space=pl.ANY)],
        [
            jax.ShapeDtypeStruct((rows, half), F32),
            jax.ShapeDtypeStruct((half // LANES, ranks, LANES), F32),
        ]
        + [pltpu.HBM((rows, half), F32)] * own,
        [IN_VMEM, IN_VMEM] + [IN_HBM] * own,
        [
            pltpu.VMEM((rows, half), F32),
            pltpu.VMEM((rows, half), F32),
            pltpu.VMEM((ranks, rows), F32),
            pltpu.SemaphoreType.DMA((3, half // CHUNK + 1)),
        ],
        6 * rows * half * ranks,
        12 * rows * half,
    )(in_hbm(pseudo_grad), in_hbm(error_buffer), in_hbm(basis_t), anchor)


def paired_product(factor, kept, arrived):
    _, ranks, _ = factor.shape
    rows, half = kept.shape
    share = jax.ShapeDtypeStruct((rows, half), BF16)
    return flat_call(
        paired_kernel,
        [IN_VMEM, IN_VMEM, IN_HBM],
        [jax.ShapeDtypeStruct((ranks, rows + LANES), F32), share, share],
        [IN_VMEM] * 3,
        [pltpu.VMEM((rows, half), F32), pltpu.SemaphoreType.DMA((half // CHUNK,))],
        6 * rows * half * ranks,
        12 * rows * half,
    )(factor, kept, in_hbm(arrived))


def near_product(factor, kept, away):
    _, ranks, _ = factor.shape
    rows, half = kept.shape
    return flat_call(
        near_kernel,
        [IN_VMEM, IN_VMEM, IN_HBM],
        [
            jax.ShapeDtypeStruct((ranks, rows), F32),
            jax.ShapeDtypeStruct((ranks, ranks), F32),
            jax.ShapeDtypeStruct((rows, half), F32),
        ],
        [IN_VMEM] * 3,
        [pltpu.SemaphoreType.DMA],
        6 * rows * half * ranks,
        8 * rows * half,
    )(factor, kept, in_hbm(away))


def far_product(factor, merged, proj_t, gram):
    _, ranks, _ = factor.shape
    rows, half = merged.shape
    return flat_call(
        far_kernel,
        [IN_VMEM] * 4,
        [jax.ShapeDtypeStruct((ranks, rows), F32), jax.ShapeDtypeStruct((ranks, ranks), F32)],
        [IN_VMEM] * 2,
        [],
        6 * rows * half * ranks,
        4 * rows * half,
    )(factor, merged, proj_t, gram)


def on_device(pseudo_grad, error_buffer, momentum, weights, warm_basis):
    _, rows, columns = pseudo_grad.shape
    ranks = warm_basis.shape[1]
    count = columns // LANES
    flops = 6 * rows * columns * ranks
    size = 4 * rows * columns
    short = whole(ranks, rows)
    square = whole(ranks, ranks)
    basis_t = warm_basis.T

    other, given = merged_half(False, pseudo_grad, error_buffer, basis_t, basis_t)
    kept, share, away = merged_half(True, pseudo_grad, error_buffer, basis_t, other)
    share = share + lax.ppermute(given, "core", SIBLING)
    share, leaving = lax.optimization_barrier((share, away))
    arrived = lax.ppermute(leaving, "core", SIBLING)
    proj_t, high_half, low_half = paired_product(over_chips(share), kept, arrived)
    paired = summed_directly(proj_t, "core")
    summed_t = summed_directly(paired[:, :rows], "y")
    inverse = inverse_factor(paired, paired, rows // LANES)
    (partial_blocks,) = call(
        partial_kernel,
        columns // 2,
        [wide(rows), wide(rows), short, square],
        [((count // 2, ranks, LANES), F32, blocks(ranks))],
        [pltpu.VMEM((ranks, rows), F32)],
        flops=flops // 2,
        traffic=size // 2,
    )(high_half, low_half, summed_t, inverse)
    near = over_chips(partial_blocks)
    far = lax.ppermute(near, "core", SIBLING)
    proj_t, gram, away = near_product(near, kept, away)
    proj_t, gram = far_product(far, away, proj_t, gram)
    paired = summed_directly(proj_t, "core")
    summed_t = summed_directly(paired, "y")
    inverse = inverse_factor(gram, paired)
    new_error, new_momentum, new_weights, basis_t = flat_call(
        finish_kernel,
        [IN_VMEM] * 9,
        [
            pltpu.HBM((1, rows, columns), F32),
            pltpu.HBM((rows, columns), F32),
            pltpu.HBM((rows, columns), BF16),
            jax.ShapeDtypeStruct((ranks, rows), F32),
        ],
        [IN_HBM] * 3 + [IN_VMEM],
        [
            pltpu.VMEM((2 * rows, 3 * ranks), BF16),
            pltpu.VMEM((rows, columns), F32),
            pltpu.VMEM((rows, columns), F32),
            pltpu.VMEM((rows, columns), BF16),
            pltpu.SemaphoreType.DMA((3, columns // CHUNK)),
        ],
        2 * flops,
        5 * size,
    )(kept, away, near, far, momentum, weights, proj_t, summed_t, inverse)
    return new_error, new_momentum, new_weights, basis_t.T


def solution(mesh):
    grid = Mesh(mesh.devices.reshape(4, 2, 4, 8), ("y", "core", "x", "z"))
    island, shard = ("y", "core"), ("x", "z")
    in_specs = (
        P(island, shard, None),
        P(island, shard, None),
        P(shard, None),
        P(shard, None),
        P(shard, None),
    )
    out_specs = (P(island, shard, None), P(shard, None), P(shard, None), P(shard, None))
    return jax.shard_map(
        on_device, mesh=grid, in_specs=in_specs, out_specs=out_specs, check_vma=False
    )
```
